32 devices in a mesh: grp: 4 (over z), mem: 8 (over y, x, core).
Axes of the slice: x: 2, y: 2, z: 4, core: 2. Of those that a mesh axis runs over, the one named last changes fastest.
Arguments:
- spectra: bfloat16 [128, 8, 2, 1024], P(('grp', 'mem')), may hold values from -6 to 6
- seg_mask: int32 [128, 8], P(('grp', 'mem')), may hold values 0 or 1
- chan_pos: int32 [128], P(('grp', 'mem')), may hold values from 0 to 127, each once
Outputs:
- correlations: bfloat16 [128, 4, 32, 128], P('grp', None, 'mem')
The draws below stay inside these ranges and needn't reach their ends.
Inputs may be any that keep to these rules, and one draw needn't show every extreme that they name: `seg_mask`: segment validity is 0 or 1. `chan_pos`: each position appears once.
All inputs are finite; a program needn't handle non-finite values. No bound on the sum of `seg_mask` on one device may be relied on, other than what follows from the above.
Results may differ from the reference program's by a relative error of at most 0.0045.
Values may be sent and summed in bfloat16 or wider, within the bound.
A program may use at most 128 MiB of HBM per device.

```python
import math
import jax
import jax.numpy as jnp
from jax import lax

BINS = 1024
LAGS = 128
SEGS = 8
CHANNELS = 128
N_GRP = 4


def with_ends(entries, own_key, least, top_value):
    place = [jax.random.randint(jax.random.fold_in(own_key, axis), (), 0, length) for axis, length in enumerate(entries.shape)]
    main_axis = entries.shape.index(max(entries.shape))
    beside = place[:main_axis] + [(place[main_axis] + 1) % entries.shape[main_axis]] + place[main_axis + 1:]
    return entries.at[tuple(place)].set(least).at[tuple(beside)].set(top_value)


def steps_of(key, extent, split, low, top_value):
    gain = 1.0
    for position, blocks in split:
        draws = jax.random.uniform(jax.random.fold_in(jax.random.fold_in(key, 6), position), (blocks,), jnp.float32, low / len(split), top_value / len(split))
        gain = gain * jnp.repeat(jnp.exp(draws), extent[position] // blocks).reshape((-1,) + (1,) * (len(extent) - 1 - position))
    return gain


def gaussian(rng, shape, deviation, most, cuts=(), kind=jnp.bfloat16):
    values = deviation * jax.random.normal(rng, shape, jnp.float32)
    if cuts:
        values = values * steps_of(rng, shape, cuts, -0.22, 0.18)
    return jnp.clip(values, -most, most).astype(kind)


def setup_inputs(seed: int = 0) -> dict:
    keys = jax.random.split(jax.random.key(seed), 4)
    return {
        "spectra": gaussian(keys[0], (CHANNELS, SEGS, 2, BINS), 1.0, 6.0, ((0, 32),)),
        "seg_mask": with_ends((jax.random.randint(keys[1], (CHANNELS, SEGS), 0, 4) < 3).astype(jnp.int32), jax.random.fold_in(keys[1], 1), 0, 1),
        "chan_pos": jax.random.permutation(keys[2], CHANNELS).astype(jnp.int32),
    }


def make_table(bins, lags):
    freq = jnp.arange(bins, dtype=jnp.int32)
    lag_ids = jnp.arange(lags, dtype=jnp.int32) - lags // 2
    phase = jnp.mod(freq[:, None] * lag_ids[None, :], bins).astype(jnp.float32) * (2.0 * math.pi / bins)
    table = jnp.concatenate([jnp.cos(phase), -jnp.sin(phase)], axis=0).astype(jnp.bfloat16)
    return (table, lag_ids.astype(jnp.float32))

def reference(spectra, seg_mask, chan_pos):
    masked = spectra * seg_mask.astype(jnp.bfloat16)[:, :, None, None]
    table, lag_vals = make_table(BINS, LAGS)
    table_wide = table.astype(jnp.float32)
    ratio = LAGS / CHANNELS
    scale = math.sqrt(BINS)
    wide = masked.astype(jnp.float32)
    flat = wide.reshape(CHANNELS, 2 * SEGS, BINS)
    turned = jnp.stack((-wide[:, :, 1], wide[:, :, 0]), axis=2).reshape(CHANNELS, 2 * SEGS, BINS)
    bstack = jnp.stack([flat, turned], axis=1)
    col_mask = seg_mask.astype(jnp.float32)
    col_pos = chan_pos.astype(jnp.float32)
    block = 16

    def one_block(args):
        spec_blk, mask_blk, pos_blk = args
        cross = jnp.einsum('itf,jctf->ijcf', spec_blk, bstack, precision=lax.Precision.HIGHEST)
        cross = lax.optimization_barrier(cross.astype(jnp.bfloat16)).astype(jnp.float32)
        raw = jnp.dot(cross.reshape(block * CHANNELS, 2 * BINS), table_wide, precision=lax.Precision.HIGHEST).reshape(block, CHANNELS, LAGS)
        count = jnp.dot(mask_blk.astype(jnp.float32), col_mask.T, precision=lax.Precision.HIGHEST)
        dist = jnp.abs(pos_blk.astype(jnp.float32)[:, None] - col_pos[None, :])
        span = 1.0 + dist * ratio
        taper = 1.0 / (1.0 + (lag_vals / span[:, :, None]) ** 2)
        norm = 1.0 / (scale * jnp.maximum(count, 1.0))
        return (raw * taper * norm[:, :, None]).astype(jnp.bfloat16)
    out = lax.map(one_block, (flat.reshape(CHANNELS // block, block, 2 * SEGS, BINS), seg_mask.reshape(CHANNELS // block, block, SEGS), chan_pos.reshape(CHANNELS // block, block)))
    return out.reshape(CHANNELS, N_GRP, CHANNELS // N_GRP, LAGS)
```

```python
import functools
import math

import jax
import jax.numpy as jnp
import ml_dtypes
import numpy as np
from jax import lax
from jax.experimental import pallas as pl
from jax.experimental.pallas import tpu as pltpu
from jax.sharding import PartitionSpec as P

LAGS = 128
LANES = 128
META = 16
MESH = pl.DeviceIdType.MESH


def make_table(bins, lags):
    freq = np.arange(bins, dtype=np.int64)
    lag_ids = np.arange(lags, dtype=np.int64) - lags // 2
    phase = np.mod(freq[:, None] * lag_ids[None, :], bins) * (2.0 * math.pi / bins)
    table = np.concatenate([np.cos(phase), -np.sin(phase)], axis=0)
    return table.astype(np.float32).astype(ml_dtypes.bfloat16)


def flip(me, other, size):
    out, bit = 0, 1
    while bit < size:
        out = out + bit * ((me // bit + other // bit) % 2)
        bit *= 2
    return out


def kernel(n_grp, n_mem, ch, segs, bins, ratio, scale, x_ref, table_hbm, out_ref,
           rows, cols, turned, meta, cross, table, row_send, row_recv, col_send, col_recv, table_sem):
    g = lax.axis_index("grp")
    m = lax.axis_index("mem")
    sub = bins // LANES
    tile = 2 * sub
    per = segs * tile
    body_rows = ch * per
    ncols = n_grp * ch

    table_copy = pltpu.make_async_copy(table_hbm, table, table_sem)
    table_copy.start()

    barrier = pltpu.get_barrier_semaphore()
    for r in range(1, n_mem):
        pl.semaphore_signal(barrier, inc=1, device_id=(g, flip(m, r, n_mem)), device_id_type=MESH)
    for k in range(1, n_grp):
        pl.semaphore_signal(barrier, inc=1, device_id=((g + k) % n_grp, m), device_id_type=MESH)
    pl.semaphore_wait(barrier, n_mem + n_grp - 2)

    row_copies = [None]
    col_copies = [None]
    for k in range(1, n_grp):
        copy = pltpu.make_async_remote_copy(
            src_ref=x_ref, dst_ref=cols.at[g], send_sem=col_send.at[k], recv_sem=col_recv.at[k],
            device_id=((g + k) % n_grp, m), device_id_type=MESH)
        copy.start()
        col_copies.append(copy)
    for r in range(1, n_mem):
        copy = pltpu.make_async_remote_copy(
            src_ref=x_ref, dst_ref=rows.at[r], send_sem=row_send.at[r], recv_sem=row_recv.at[r],
            device_id=(g, flip(m, r, n_mem)), device_id_type=MESH)
        copy.start()
        row_copies.append(copy)

    def prepare(slot):
        def turn(t, carry):
            x = cols[slot, pl.ds(pl.multiple_of(t * tile, tile), tile), :].astype(jnp.float32)
            y = jnp.concatenate([-x[sub:], x[:sub]], axis=0).astype(jnp.bfloat16)
            turned[slot, pl.ds(pl.multiple_of(t * tile, tile), tile), :] = y
            return carry
        lax.fori_loop(0, ch * segs, turn, 0, unroll=8)

    rows[0] = x_ref[...]
    cols[pl.ds(g, 1)] = x_ref[...][None]
    prepare(g)
    for k in range(1, n_grp):
        col_copies[k].wait_recv()
        prepare((g + n_grp - k) % n_grp)
    for q in range(n_grp):
        meta[q * ch:(q + 1) * ch, :] = cols[q, body_rows:body_rows + META, :].astype(jnp.float32)[:ch]
    table_copy.wait()

    lane = lax.broadcasted_iota(jnp.int32, (1, LANES), 1)
    seg_lane = jnp.where(lane < segs, 1.0, 0.0)
    pos_lane = jnp.where(lane == segs, 128.0, 0.0) + jnp.where(lane == segs + 1, 1.0, 0.0)
    lag = (lax.broadcasted_iota(jnp.int32, (1, LAGS), 1) - LAGS // 2).astype(jnp.float32)
    lag2 = lag * lag

    def total(parts):
        quads = []
        for at in range(0, segs, 4):
            quad = parts[at:at + 4]
            while len(quad) > 1:
                quad = [quad[k] + quad[k + 1] if k + 1 < len(quad) else quad[k]
                        for k in range(0, len(quad), 2)]
            quads.append(quad[0].astype(jnp.float32))
        acc = quads[0]
        for one in quads[1:]:
            acc = acc + one
        return acc[:sub] + acc[sub:]

    def step(r, carry):
        @pl.when(r > 0)
        def _():
            pltpu.make_async_remote_copy(
                src_ref=x_ref, dst_ref=rows.at[r], send_sem=row_send.at[r], recv_sem=row_recv.at[r],
                device_id=(g, flip(m, r, n_mem)), device_id_type=MESH).wait_recv()

        def one_col(j, c2):
            slot = j // ch
            base = (j % ch) * per
            q, t = [], []
            for s in range(segs):
                at = pl.ds(pl.multiple_of(base + s * tile, tile), tile)
                q.append(cols[slot, at, :])
                t.append(turned[slot, at, :])
            for i in range(ch):
                p = [rows[r, i * per + s * tile:i * per + (s + 1) * tile, :] for s in range(segs)]
                at = pl.multiple_of((i * ncols + j) * tile, tile)
                cross[pl.ds(at, sub), :] = total([a * b for a, b in zip(p, q)])
                cross[pl.ds(at + sub, sub), :] = total([a * b for a, b in zip(p, t)])
            return c2

        lax.fori_loop(0, ncols, one_col, 0, unroll=2)
        raw = jnp.zeros((ch * ncols, LAGS), jnp.float32)
        for k in range(0, tile, 2):
            left = jnp.concatenate(
                [cross[pl.ds(k + d, ch * ncols, stride=tile), :].astype(jnp.bfloat16) for d in range(2)], axis=1)
            raw = raw + jnp.dot(left, table[k * LANES:(k + 2) * LANES, :], preferred_element_type=jnp.float32)
        mine = rows[r, body_rows:body_rows + META, :].astype(jnp.float32)
        theirs = meta[...]
        pos_j = jnp.sum(theirs * pos_lane, axis=1, keepdims=True)
        start = flip(m, r, n_mem) * ch
        for i in range(ch):
            one = mine[i:i + 1]
            count = jnp.sum(theirs * (one * seg_lane), axis=1, keepdims=True)
            pos_i = jnp.sum(one * pos_lane, axis=1, keepdims=True)
            span = 1.0 + jnp.abs(pos_i - pos_j) * ratio
            span2 = span * span
            factor = span2 / ((span2 + lag2) * (scale * jnp.maximum(count, 1.0)))
            out_ref[start + i] = (raw[i * ncols:(i + 1) * ncols] * factor).astype(jnp.bfloat16)
        return carry

    lax.fori_loop(0, n_mem, step, 0)

    for copy in row_copies[1:] + col_copies[1:]:
        copy.wait_send()


def body(spectra, seg_mask, chan_pos):
    ch, segs, _, bins = spectra.shape
    n_grp, n_mem = lax.axis_size("grp"), lax.axis_size("mem")
    masked = spectra * seg_mask.astype(jnp.bfloat16)[:, :, None, None]
    flat = masked.reshape(-1, LANES)
    notes = jnp.concatenate(
        [seg_mask, (chan_pos // 128)[:, None], (chan_pos % 128)[:, None]], axis=1).astype(jnp.bfloat16)
    notes = jnp.pad(notes, ((0, META - ch), (0, LANES - segs - 2)))
    message = jnp.concatenate([flat, notes], axis=0)
    size = message.shape[0]
    ncols = n_grp * ch
    out = pl.pallas_call(
        functools.partial(kernel, n_grp, n_mem, ch, segs, bins, LAGS / (ch * n_grp * n_mem), math.sqrt(bins)),
        out_shape=jax.ShapeDtypeStruct((n_mem * ch, ncols, LAGS), jnp.bfloat16),
        in_specs=[pl.BlockSpec(memory_space=pltpu.VMEM), pl.BlockSpec(memory_space=pl.ANY)],
        out_specs=pl.BlockSpec(memory_space=pltpu.VMEM),
        scratch_shapes=[
            pltpu.VMEM((n_mem, size, LANES), jnp.bfloat16),
            pltpu.VMEM((n_grp, size, LANES), jnp.bfloat16),
            pltpu.VMEM((n_grp, size, LANES), jnp.bfloat16),
            pltpu.VMEM((ncols, LANES), jnp.float32),
            pltpu.VMEM((ch * ncols * 2 * (bins // LANES), LANES), jnp.float32),
            pltpu.VMEM((2 * bins, LAGS), jnp.bfloat16),
            pltpu.SemaphoreType.DMA((n_mem,)),
            pltpu.SemaphoreType.DMA((n_mem,)),
            pltpu.SemaphoreType.DMA((n_grp,)),
            pltpu.SemaphoreType.DMA((n_grp,)),
            pltpu.SemaphoreType.DMA,
        ],
        compiler_params=pltpu.CompilerParams(
            collective_id=0, has_side_effects=True, vmem_limit_bytes=48 * 1024 * 1024),
    )(message, jnp.asarray(make_table(bins, LAGS)))
    return out.reshape(n_mem * ch, n_grp, ch, LAGS)


def solution(mesh):
    in_specs = (P(("grp", "mem"), None, None, None), P(("grp", "mem"), None), P(("grp", "mem")))
    out_specs = P("grp", None, "mem", None)
    return jax.shard_map(body, mesh=mesh, in_specs=in_specs, out_specs=out_specs, check_vma=False)
```

```python
import functools
import math

import jax
import jax.numpy as jnp
import ml_dtypes
import numpy as np
from jax import lax
from jax.experimental import pallas as pl
from jax.experimental.pallas import tpu as pltpu
from jax.sharding import PartitionSpec as P

LAGS = 128
LANES = 128
META = 16
MESH = pl.DeviceIdType.MESH


def make_table(bins, lags):
    freq = np.arange(bins, dtype=np.int64)
    lag_ids = np.arange(lags, dtype=np.int64) - lags // 2
    phase = np.mod(freq[:, None] * lag_ids[None, :], bins) * (2.0 * math.pi / bins)
    table = np.concatenate([np.cos(phase), -np.sin(phase)], axis=0)
    return table.astype(np.float32).astype(ml_dtypes.bfloat16)


def flip(me, other, size):
    out, bit = 0, 1
    while bit < size:
        out = out + bit * ((me // bit + other // bit) % 2)
        bit *= 2
    return out


def kernel(n_grp, n_mem, ch, segs, bins, ratio, scale, x_ref, mask_ref, pos_ref, table_hbm, out_ref,
           rows, cols, turned, meta, cross, table, row_send, row_recv, col_send, col_recv, table_sem):
    g = lax.axis_index("grp")
    m = lax.axis_index("mem")
    sub = bins // LANES
    tile = 2 * sub
    per = segs * tile
    body_rows = ch * per
    pairs = n_mem * ch * ch

    barrier = pltpu.get_barrier_semaphore()
    partners = [1] + list(range(2, n_mem, 2))
    for r in partners:
        pl.semaphore_signal(barrier, inc=1, device_id=(g, flip(m, r, n_mem)), device_id_type=MESH)
    for k in range(1, n_grp):
        pl.semaphore_signal(barrier, inc=1, device_id=(flip(g, k, n_grp), m), device_id_type=MESH)

    table_copy = pltpu.make_async_copy(table_hbm, table, table_sem)
    table_copy.start()

    lane = lax.broadcasted_iota(jnp.int32, (1, LANES), 1)

    def turn(slot, t, x):
        y = jnp.concatenate([-x[sub:], x[:sub]], axis=0).astype(jnp.bfloat16)
        turned[slot, pl.ds(pl.multiple_of(t * tile, tile), tile), :] = y

    notes = []
    for c in range(ch):
        place = pos_ref[c]
        note = jnp.where(lane == segs, (place // 128).astype(jnp.float32), 0.0)
        note = jnp.where(lane == segs + 1, (place % 128).astype(jnp.float32), note)
        for s in range(segs):
            valid = mask_ref[c, s].astype(jnp.float32)
            note = jnp.where(lane == s, valid, note)
            t = c * segs + s
            x = x_ref[t * tile:(t + 1) * tile, :].astype(jnp.float32) * valid
            packed = x.astype(jnp.bfloat16)
            rows[0, t * tile:(t + 1) * tile, :] = packed
            cols[0, t * tile:(t + 1) * tile, :] = packed
            turn(0, t, x)
        notes.append(note)
    notes.append(jnp.zeros((META - ch, LANES), jnp.float32))
    rows[0, body_rows:, :] = jnp.concatenate(notes, axis=0).astype(jnp.bfloat16)
    cols[0, body_rows:, :] = jnp.concatenate(notes, axis=0).astype(jnp.bfloat16)

    pl.semaphore_wait(barrier, len(partners) + n_grp - 1)

    def row_copy(r, src, to):
        return pltpu.make_async_remote_copy(
            src_ref=rows.at[src], dst_ref=rows.at[r], send_sem=row_send.at[r], recv_sem=row_recv.at[r],
            device_id=(g, flip(m, to, n_mem)), device_id_type=MESH)

    def col_copy(k):
        return pltpu.make_async_remote_copy(
            src_ref=rows.at[0], dst_ref=cols.at[k], send_sem=col_send.at[k], recv_sem=col_recv.at[k],
            device_id=(flip(g, k, n_grp), m), device_id_type=MESH)

    for k in range(1, n_grp):
        col_copy(k).start()
    for r in partners[1:]:
        row_copy(r, 0, r).start()
    row_copy(1, 0, 1).start()

    pos_lane = jnp.where(lane == segs, 128.0, 0.0) + jnp.where(lane == segs + 1, 1.0, 0.0)
    seg_lane = jnp.where(lane < segs, 1.0, 0.0)
    lag = (lax.broadcasted_iota(jnp.int32, (1, LAGS), 1) - LAGS // 2).astype(jnp.float32)
    lag2 = lag * lag

    def total(parts):
        quads = []
        for at in range(0, segs, 4):
            quad = parts[at:at + 4]
            while len(quad) > 1:
                quad = [quad[k] + quad[k + 1] if k + 1 < len(quad) else quad[k]
                        for k in range(0, len(quad), 2)]
            quads.append(quad[0].astype(jnp.float32))
        acc = quads[0]
        for one in quads[1:]:
            acc = acc + one
        return acc[:sub] + acc[sub:]

    def block(r, k):
        def one_col(j, carry):
            base = j * per
            q, t = [], []
            for s in range(segs):
                at = pl.ds(pl.multiple_of(base + s * tile, tile), tile)
                q.append(cols[k, at, :])
                t.append(turned[k, at, :])
            for i in range(ch):
                p = [rows[r, i * per + s * tile:i * per + (s + 1) * tile, :] for s in range(segs)]
                at = pl.multiple_of(((r * ch + i) * ch + j) * tile, tile)
                cross[pl.ds(at, sub), :] = total([a * b for a, b in zip(p, q)])
                cross[pl.ds(at + sub, sub), :] = total([a * b for a, b in zip(p, t)])
            return carry
        lax.fori_loop(0, ch, one_col, 0, unroll=4)

    def expand(r):
        mine = rows[r, body_rows:body_rows + META, :].astype(jnp.float32)
        wide = jnp.concatenate(
            [jnp.broadcast_to(mine[i:i + 1], (ch, LANES)) for i in range(ch)], axis=0)
        meta[pl.ds(pl.multiple_of(r * ch * ch, ch * ch), ch * ch), :] = wide

    def finish(k):
        raw = jnp.zeros((pairs, LAGS), jnp.float32)
        for at in range(0, tile, 2):
            left = jnp.concatenate(
                [cross[pl.ds(at + d, pairs, stride=tile), :].astype(jnp.bfloat16) for d in range(2)], axis=1)
            raw = raw + jnp.dot(left, table[at * LANES:(at + 2) * LANES, :], preferred_element_type=jnp.float32)
        theirs = cols[k, body_rows:body_rows + META, :].astype(jnp.float32)[:ch]
        theirs = jnp.concatenate([theirs] * (n_mem * ch), axis=0)
        mine = meta[...]
        count = jnp.sum(theirs * mine * seg_lane, axis=1, keepdims=True)
        dist = jnp.abs(jnp.sum((theirs - mine) * pos_lane, axis=1, keepdims=True))
        span = 1.0 + dist * ratio
        span2 = span * span
        factor = span2 / ((span2 + lag2) * (scale * jnp.maximum(count, 1.0)))
        out = (raw * factor).reshape(n_mem, ch, ch, LAGS).astype(jnp.bfloat16)
        source = flip(g, k, n_grp)
        for r in range(n_mem):
            start = flip(m, r, n_mem) * ch
            for i in range(ch):
                out_ref[start + i, source] = out[r, i]

    def first(r, carry):
        @pl.when(r > 0)
        def _():
            row_copy(r, 0, r).wait_recv()

        @pl.when((r > 1) & (r % 2 == 0))
        def _():
            row_copy(r + 1, r, 1).start()

        expand(r)
        block(r, 0)
        return carry

    lax.fori_loop(0, n_mem, first, 0)
    table_copy.wait()
    finish(0)

    def later(k, carry):
        col_copy(k).wait_recv()

        def prepare(t, c2):
            turn(k, t, cols[k, pl.ds(pl.multiple_of(t * tile, tile), tile), :].astype(jnp.float32))
            return c2

        def rest(r, c2):
            block(r, k)
            return c2

        lax.fori_loop(0, ch * segs, prepare, 0, unroll=8)
        lax.fori_loop(0, n_mem, rest, 0)
        finish(k)
        return carry

    lax.fori_loop(1, n_grp, later, 0)

    for r in range(1, n_mem):
        row_copy(r, 0, r).wait_send()
    for k in range(1, n_grp):
        col_copy(k).wait_send()


def body(spectra, seg_mask, chan_pos):
    ch, segs, _, bins = spectra.shape
    n_grp, n_mem = lax.axis_size("grp"), lax.axis_size("mem")
    flat = spectra.reshape(-1, LANES)
    size = flat.shape[0] + META
    out = pl.pallas_call(
        functools.partial(kernel, n_grp, n_mem, ch, segs, bins, LAGS / (ch * n_grp * n_mem), math.sqrt(bins)),
        out_shape=jax.ShapeDtypeStruct((n_mem * ch, n_grp, ch, LAGS), jnp.bfloat16),
        in_specs=[
            pl.BlockSpec(memory_space=pltpu.VMEM),
            pl.BlockSpec(memory_space=pltpu.SMEM),
            pl.BlockSpec(memory_space=pltpu.SMEM),
            pl.BlockSpec(memory_space=pl.ANY),
        ],
        out_specs=pl.BlockSpec(memory_space=pltpu.VMEM),
        scratch_shapes=[
            pltpu.VMEM((n_mem, size, LANES), jnp.bfloat16),
            pltpu.VMEM((n_grp, size, LANES), jnp.bfloat16),
            pltpu.VMEM((n_grp, size, LANES), jnp.bfloat16),
            pltpu.VMEM((n_mem * ch * ch, LANES), jnp.float32),
            pltpu.VMEM((n_mem * ch * ch * 2 * (bins // LANES), LANES), jnp.float32),
            pltpu.VMEM((2 * bins, LAGS), jnp.bfloat16),
            pltpu.SemaphoreType.DMA((n_mem,)),
            pltpu.SemaphoreType.DMA((n_mem,)),
            pltpu.SemaphoreType.DMA((n_grp,)),
            pltpu.SemaphoreType.DMA((n_grp,)),
            pltpu.SemaphoreType.DMA,
        ],
        compiler_params=pltpu.CompilerParams(
            collective_id=0, has_side_effects=True, vmem_limit_bytes=48 * 1024 * 1024),
    )(flat, seg_mask, chan_pos, jnp.asarray(make_table(bins, LAGS)))
    return out


def solution(mesh):
    in_specs = (P(("grp", "mem"), None, None, None), P(("grp", "mem"), None), P(("grp", "mem")))
    out_specs = P("grp", None, "mem", None)
    return jax.shard_map(body, mesh=mesh, in_specs=in_specs, out_specs=out_specs, check_vma=False)
```

```python
import functools
import math

import jax
import jax.numpy as jnp
import ml_dtypes
import numpy as np
from jax import lax
from jax.experimental import pallas as pl
from jax.experimental.pallas import tpu as pltpu
from jax.sharding import PartitionSpec as P

LAGS = 128
LANES = 128
META = 16
MESH = pl.DeviceIdType.MESH


def make_table(bins, lags):
    freq = np.arange(bins, dtype=np.int64)
    lag_ids = np.arange(lags, dtype=np.int64) - lags // 2
    phase = np.mod(freq[:, None] * lag_ids[None, :], bins) * (2.0 * math.pi / bins)
    table = np.concatenate([np.cos(phase), -np.sin(phase)], axis=0)
    return table.astype(np.float32).astype(ml_dtypes.bfloat16)


def flip(me, other, size):
    out, bit = 0, 1
    while bit < size:
        out = out + bit * ((me // bit + other // bit) % 2)
        bit *= 2
    return out


def kernel(n_grp, n_mem, ch, segs, bins, ratio, scale, x_ref, mask_ref, pos_ref, table_hbm, out_ref,
           rows, cols, turned, meta, cross, table, row_send, row_recv, col_send, col_recv, table_sem):
    g = lax.axis_index("grp")
    m = lax.axis_index("mem")
    sub = bins // LANES
    tile = 2 * sub
    per = segs * tile
    body_rows = ch * per
    pairs = n_mem * ch * ch

    barrier = pltpu.get_barrier_semaphore()
    partners = [1] + list(range(2, n_mem, 2))
    for r in partners:
        pl.semaphore_signal(barrier, inc=1, device_id=(g, flip(m, r, n_mem)), device_id_type=MESH)
    for k in range(1, n_grp):
        pl.semaphore_signal(barrier, inc=1, device_id=(flip(g, k, n_grp), m), device_id_type=MESH)

    table_copy = pltpu.make_async_copy(table_hbm, table, table_sem)
    table_copy.start()

    lane = lax.broadcasted_iota(jnp.int32, (1, LANES), 1)

    def turn(slot, t, x):
        y = jnp.concatenate([-x[sub:], x[:sub]], axis=0).astype(jnp.bfloat16)
        turned[slot, pl.ds(pl.multiple_of(t * tile, tile), tile), :] = y

    notes = []
    for c in range(ch):
        place = pos_ref[c]
        note = jnp.where(lane == segs, (place // 128).astype(jnp.float32), 0.0)
        note = jnp.where(lane == segs + 1, (place % 128).astype(jnp.float32), note)
        for s in range(segs):
            valid = mask_ref[c, s].astype(jnp.float32)
            note = jnp.where(lane == s, valid, note)
            t = c * segs + s
            x = x_ref[t * tile:(t + 1) * tile, :].astype(jnp.float32) * valid
            packed = x.astype(jnp.bfloat16)
            rows[0, t * tile:(t + 1) * tile, :] = packed
            cols[0, t * tile:(t + 1) * tile, :] = packed
            turn(0, t, x)
        notes.append(note)
    notes.append(jnp.zeros((META - ch, LANES), jnp.float32))
    rows[0, body_rows:, :] = jnp.concatenate(notes, axis=0).astype(jnp.bfloat16)
    cols[0, body_rows:, :] = jnp.concatenate(notes, axis=0).astype(jnp.bfloat16)

    pl.semaphore_wait(barrier, len(partners) + n_grp - 1)

    def row_copy(r, src, to):
        return pltpu.make_async_remote_copy(
            src_ref=rows.at[src], dst_ref=rows.at[r], send_sem=row_send.at[r], recv_sem=row_recv.at[r],
            device_id=(g, flip(m, to, n_mem)), device_id_type=MESH)

    def col_copy(k):
        return pltpu.make_async_remote_copy(
            src_ref=rows.at[0], dst_ref=cols.at[k], send_sem=col_send.at[k], recv_sem=col_recv.at[k],
            device_id=(flip(g, k, n_grp), m), device_id_type=MESH)

    relay = n_grp == 4
    middle = (g > 0) & (g < n_grp - 1)
    passed = pltpu.make_async_remote_copy(
        src_ref=cols.at[n_grp // 2], dst_ref=cols.at[n_grp - 1], send_sem=col_send.at[0],
        recv_sem=col_recv.at[n_grp - 1], device_id=(flip(g, 1, n_grp), m), device_id_type=MESH)

    if relay:
        col_copy(2).start()
        col_copy(1).start()

        @pl.when(middle)
        def _():
            col_copy(3).start()
    else:
        for k in range(1, n_grp):
            col_copy(k).start()
    for r in partners[1:]:
        row_copy(r, 0, r).start()
    row_copy(1, 0, 1).start()

    pos_lane = jnp.where(lane == segs, 128.0, 0.0) + jnp.where(lane == segs + 1, 1.0, 0.0)
    seg_lane = jnp.where(lane < segs, 1.0, 0.0)
    lag = (lax.broadcasted_iota(jnp.int32, (1, LAGS), 1) - LAGS // 2).astype(jnp.float32)
    lag2 = lag * lag

    def total(parts):
        quads = []
        for at in range(0, segs, 4):
            quad = parts[at:at + 4]
            while len(quad) > 1:
                quad = [quad[k] + quad[k + 1] if k + 1 < len(quad) else quad[k]
                        for k in range(0, len(quad), 2)]
            quads.append(quad[0].astype(jnp.float32))
        acc = quads[0]
        for one in quads[1:]:
            acc = acc + one
        return acc[:sub] + acc[sub:]

    def block(r, k, slot):
        def one_col(j, carry):
            base = j * per
            q, t = [], []
            for s in range(segs):
                at = pl.ds(pl.multiple_of(base + s * tile, tile), tile)
                q.append(cols[k, at, :])
                t.append(turned[k, at, :])
            for i in range(ch):
                p = [rows[r, i * per + s * tile:i * per + (s + 1) * tile, :] for s in range(segs)]
                at = pl.multiple_of((((slot * n_mem + r) * ch + i) * ch + j) * tile, tile)
                cross[pl.ds(at, sub), :] = total([a * b for a, b in zip(p, q)])
                cross[pl.ds(at + sub, sub), :] = total([a * b for a, b in zip(p, t)])
            return carry
        lax.fori_loop(0, ch, one_col, 0, unroll=4)

    def expand(r):
        mine = rows[r, body_rows:body_rows + META, :].astype(jnp.float32)
        wide = jnp.concatenate(
            [jnp.broadcast_to(mine[i:i + 1], (ch, LANES)) for i in range(ch)], axis=0)
        meta[pl.ds(pl.multiple_of(r * ch * ch, ch * ch), ch * ch), :] = wide

    def finish(k, slot):
        raw = jnp.zeros((pairs, LAGS), jnp.float32)
        for at in range(0, tile, 2):
            left = jnp.concatenate(
                [cross[pl.ds(slot * pairs * tile + at + d, pairs, stride=tile), :].astype(jnp.bfloat16) for d in range(2)], axis=1)
            raw = raw + jnp.dot(left, table[at * LANES:(at + 2) * LANES, :], preferred_element_type=jnp.float32)
        theirs = cols[k, body_rows:body_rows + META, :].astype(jnp.float32)[:ch]
        theirs = jnp.concatenate([theirs] * (n_mem * ch), axis=0)
        mine = meta[...]
        count = jnp.sum(theirs * mine * seg_lane, axis=1, keepdims=True)
        dist = jnp.abs(jnp.sum((theirs - mine) * pos_lane, axis=1, keepdims=True))
        span = 1.0 + dist * ratio
        span2 = span * span
        factor = span2 / ((span2 + lag2) * (scale * jnp.maximum(count, 1.0)))
        out = (raw * factor).reshape(n_mem, ch, ch, LAGS).astype(jnp.bfloat16)
        source = flip(g, k, n_grp)
        for r in range(n_mem):
            start = flip(m, r, n_mem) * ch
            for i in range(ch):
                out_ref[start + i, source] = out[r, i]

    def prepare(k):
        def one(t, carry):
            turn(k, t, cols[k, pl.ds(pl.multiple_of(t * tile, tile), tile), :].astype(jnp.float32))
            return carry

        lax.fori_loop(0, ch * segs, one, 0, unroll=8)

    def blocks(low, high, k, slot):
        def one(r, carry):
            block(r, k, slot)
            return carry

        lax.fori_loop(low, high, one, 0)

    expand(0)
    row_copy(1, 0, 1).wait_recv()
    expand(1)
    blocks(0, 2, 0, 0)
    col_copy(1).wait_recv()
    prepare(1)
    blocks(0, 2, 1, 1)
    table_copy.wait()
    half = n_mem // 2 - 1

    def hand_on():
        col_copy(2).wait_recv()

        @pl.when(middle)
        def _():
            passed.start()

    def arrive(e, carry):
        if relay:
            @pl.when(e == min(2, half))
            def _():
                hand_on()

        r = 2 + 2 * (e % half) + e // half
        row_copy(r, 0, r).wait_recv()

        @pl.when(e < half)
        def _():
            row_copy(r + 1, r, 1).start()

        expand(r)

        def near(k, c2):
            block(r, k, k)
            return c2

        lax.fori_loop(0, 2, near, 0)
        return carry

    if half:
        lax.fori_loop(0, 2 * half, arrive, 0)
    elif relay:
        hand_on()
    finish(0, 0)
    finish(1, 1)

    def later(k, carry):
        if relay:
            @pl.when(k > 2)
            def _():
                col_copy(k).wait_recv()
        else:
            col_copy(k).wait_recv()
        prepare(k)
        blocks(0, n_mem, k, 0)
        finish(k, 0)
        return carry

    lax.fori_loop(2, n_grp, later, 0)

    for r in range(1, n_mem):
        row_copy(r, 0, r).wait_send()
    if relay:
        col_copy(1).wait_send()
        col_copy(2).wait_send()

        @pl.when(middle)
        def _():
            col_copy(3).wait_send()
            passed.wait_send()
    else:
        for k in range(1, n_grp):
            col_copy(k).wait_send()


def body(spectra, seg_mask, chan_pos):
    ch, segs, _, bins = spectra.shape
    n_grp, n_mem = lax.axis_size("grp"), lax.axis_size("mem")
    flat = spectra.reshape(-1, LANES)
    size = flat.shape[0] + META
    out = pl.pallas_call(
        functools.partial(kernel, n_grp, n_mem, ch, segs, bins, LAGS / (ch * n_grp * n_mem), math.sqrt(bins)),
        out_shape=jax.ShapeDtypeStruct((n_mem * ch, n_grp, ch, LAGS), jnp.bfloat16),
        in_specs=[
            pl.BlockSpec(memory_space=pltpu.VMEM),
            pl.BlockSpec(memory_space=pltpu.SMEM),
            pl.BlockSpec(memory_space=pltpu.SMEM),
            pl.BlockSpec(memory_space=pltpu.HBM),
        ],
        out_specs=pl.BlockSpec(memory_space=pltpu.VMEM),
        scratch_shapes=[
            pltpu.VMEM((n_mem, size, LANES), jnp.bfloat16),
            pltpu.VMEM((n_grp, size, LANES), jnp.bfloat16),
            pltpu.VMEM((n_grp, size, LANES), jnp.bfloat16),
            pltpu.VMEM((n_mem * ch * ch, LANES), jnp.float32),
            pltpu.VMEM((2 * n_mem * ch * ch * 2 * (bins // LANES), LANES), jnp.float32),
            pltpu.VMEM((2 * bins, LAGS), jnp.bfloat16),
            pltpu.SemaphoreType.DMA((n_mem,)),
            pltpu.SemaphoreType.DMA((n_mem,)),
            pltpu.SemaphoreType.DMA((n_grp,)),
            pltpu.SemaphoreType.DMA((n_grp,)),
            pltpu.SemaphoreType.DMA,
        ],
        compiler_params=pltpu.CompilerParams(
            collective_id=0, has_side_effects=True, vmem_limit_bytes=48 * 1024 * 1024),
    )(flat, seg_mask, chan_pos, jnp.asarray(make_table(bins, LAGS)))
    return out


def solution(mesh):
    in_specs = (P(("grp", "mem"), None, None, None), P(("grp", "mem"), None), P(("grp", "mem")))
    out_specs = P("grp", None, "mem", None)
    return jax.shard_map(body, mesh=mesh, in_specs=in_specs, out_specs=out_specs, check_vma=False)
```

```python
import functools
import math

import jax
import jax.numpy as jnp
import ml_dtypes
import numpy as np
from jax import lax
from jax.experimental import pallas as pl
from jax.experimental.pallas import tpu as pltpu
from jax.sharding import PartitionSpec as P

LAGS = 128
LANES = 128
META = 16
MESH = pl.DeviceIdType.MESH


def make_table(bins, lags):
    freq = np.arange(bins, dtype=np.int64)
    lag_ids = np.arange(lags, dtype=np.int64) - lags // 2
    phase = np.mod(freq[:, None] * lag_ids[None, :], bins) * (2.0 * math.pi / bins)
    table = np.concatenate([np.cos(phase), -np.sin(phase)], axis=0)
    return table.astype(np.float32).astype(ml_dtypes.bfloat16)


def flip(me, other, size):
    out, bit = 0, 1
    while bit < size:
        out = out + bit * ((me // bit + other // bit) % 2)
        bit *= 2
    return out


def kernel(n_grp, n_mem, ch, segs, bins, ratio, scale, x_ref, mask_ref, pos_ref, table_hbm, out_ref,
           rows, cols, turned, meta, cross, table, row_send, row_recv, col_send, col_recv, table_sem):
    g = lax.axis_index("grp")
    m = lax.axis_index("mem")
    sub = bins // LANES
    tile = 2 * sub
    per = segs * tile
    body_rows = ch * per
    pairs = n_mem * ch * ch

    barrier = pltpu.get_barrier_semaphore()
    partners = [1] + list(range(2, n_mem, 2))
    for r in partners:
        pl.semaphore_signal(barrier, inc=1, device_id=(g, flip(m, r, n_mem)), device_id_type=MESH)
    for k in range(1, n_grp):
        pl.semaphore_signal(barrier, inc=1, device_id=(flip(g, k, n_grp), m), device_id_type=MESH)

    table_copy = pltpu.make_async_copy(table_hbm, table, table_sem)
    table_copy.start()

    lane = lax.broadcasted_iota(jnp.int32, (1, LANES), 1)

    def turn(slot, t, x):
        y = jnp.concatenate([-x[sub:], x[:sub]], axis=0).astype(jnp.bfloat16)
        turned[slot, pl.ds(pl.multiple_of(t * tile, tile), tile), :] = y

    notes = []
    for c in range(ch):
        place = pos_ref[c]
        note = jnp.where(lane == segs, (place // 128).astype(jnp.float32), 0.0)
        note = jnp.where(lane == segs + 1, (place % 128).astype(jnp.float32), note)
        for s in range(segs):
            valid = mask_ref[c, s].astype(jnp.float32)
            note = jnp.where(lane == s, valid, note)
            t = c * segs + s
            x = x_ref[t * tile:(t + 1) * tile, :].astype(jnp.float32) * valid
            packed = x.astype(jnp.bfloat16)
            rows[0, t * tile:(t + 1) * tile, :] = packed
            cols[0, t * tile:(t + 1) * tile, :] = packed
            turn(0, t, x)
        notes.append(note)
    notes.append(jnp.zeros((META - ch, LANES), jnp.float32))
    rows[0, body_rows:, :] = jnp.concatenate(notes, axis=0).astype(jnp.bfloat16)
    cols[0, body_rows:, :] = jnp.concatenate(notes, axis=0).astype(jnp.bfloat16)

    pl.semaphore_wait(barrier, len(partners) + n_grp - 1)

    def row_copy(r, src, to):
        return pltpu.make_async_remote_copy(
            src_ref=rows.at[src], dst_ref=rows.at[r], send_sem=row_send.at[r], recv_sem=row_recv.at[r],
            device_id=(g, flip(m, to, n_mem)), device_id_type=MESH)

    def col_copy(k):
        return pltpu.make_async_remote_copy(
            src_ref=rows.at[0], dst_ref=cols.at[k], send_sem=col_send.at[k], recv_sem=col_recv.at[k],
            device_id=(flip(g, k, n_grp), m), device_id_type=MESH)

    relay = n_grp == 4
    middle = (g > 0) & (g < n_grp - 1)
    passed = pltpu.make_async_remote_copy(
        src_ref=cols.at[n_grp // 2], dst_ref=cols.at[n_grp - 1], send_sem=col_send.at[0],
        recv_sem=col_recv.at[n_grp - 1], device_id=(flip(g, 1, n_grp), m), device_id_type=MESH)

    if relay:
        col_copy(2).start()
        col_copy(1).start()

        @pl.when(middle)
        def _():
            col_copy(3).start()
    else:
        for k in range(1, n_grp):
            col_copy(k).start()
    for r in partners[1:]:
        row_copy(r, 0, r).start()
    row_copy(1, 0, 1).start()

    pos_lane = jnp.where(lane == segs, 128.0, 0.0) + jnp.where(lane == segs + 1, 1.0, 0.0)
    seg_lane = jnp.where(lane < segs, 1.0, 0.0)
    lag = (lax.broadcasted_iota(jnp.int32, (1, LAGS), 1) - LAGS // 2).astype(jnp.float32)
    lag2 = lag * lag

    def total(parts):
        quads = []
        for at in range(0, segs, 4):
            quad = parts[at:at + 4]
            while len(quad) > 1:
                quad = [quad[k] + quad[k + 1] if k + 1 < len(quad) else quad[k]
                        for k in range(0, len(quad), 2)]
            quads.append(quad[0].astype(jnp.float32))
        acc = quads[0]
        for one in quads[1:]:
            acc = acc + one
        return acc[:sub] + acc[sub:]

    def block(r, k, slot):
        def one_col(j, carry):
            base = j * per
            q, t = [], []
            for s in range(segs):
                at = pl.ds(pl.multiple_of(base + s * tile, tile), tile)
                q.append(cols[k, at, :])
                t.append(turned[k, at, :])
            for i in range(ch):
                p = [rows[r, i * per + s * tile:i * per + (s + 1) * tile, :] for s in range(segs)]
                at = pl.multiple_of((((slot * n_mem + r) * ch + i) * ch + j) * tile, tile)
                cross[pl.ds(at, sub), :] = total([a * b for a, b in zip(p, q)])
                cross[pl.ds(at + sub, sub), :] = total([a * b for a, b in zip(p, t)])
            return carry
        lax.fori_loop(0, ch, one_col, 0, unroll=4)

    def expand(r):
        mine = rows[r, body_rows:body_rows + META, :].astype(jnp.float32)
        wide = jnp.concatenate(
            [jnp.broadcast_to(mine[i:i + 1], (ch, LANES)) for i in range(ch)], axis=0)
        meta[pl.ds(pl.multiple_of(r * ch * ch, ch * ch), ch * ch), :] = wide

    def finish(k, slot):
        raw = jnp.zeros((pairs, LAGS), jnp.float32)
        for at in range(0, tile, 2):
            left = jnp.concatenate(
                [cross[pl.ds(slot * pairs * tile + at + d, pairs, stride=tile), :].astype(jnp.bfloat16) for d in range(2)], axis=1)
            raw = raw + jnp.dot(left, table[at * LANES:(at + 2) * LANES, :], preferred_element_type=jnp.float32)
        theirs = cols[k, body_rows:body_rows + META, :].astype(jnp.float32)[:ch]
        theirs = jnp.concatenate([theirs] * (n_mem * ch), axis=0)
        mine = meta[...]
        count = jnp.sum(theirs * mine * seg_lane, axis=1, keepdims=True)
        dist = jnp.abs(jnp.sum((theirs - mine) * pos_lane, axis=1, keepdims=True))
        span = 1.0 + dist * ratio
        span2 = span * span
        factor = span2 / ((span2 + lag2) * (scale * jnp.maximum(count, 1.0)))
        out = (raw * factor).reshape(n_mem, ch, ch, LAGS).astype(jnp.bfloat16)
        source = flip(g, k, n_grp)
        for r in range(n_mem):
            start = flip(m, r, n_mem) * ch
            for i in range(ch):
                out_ref[start + i, source] = out[r, i]

    def prepare(k):
        def one(t, carry):
            turn(k, t, cols[k, pl.ds(pl.multiple_of(t * tile, tile), tile), :].astype(jnp.float32))
            return carry

        lax.fori_loop(0, ch * segs, one, 0, unroll=8)

    def blocks(low, high, k, slot):
        def one(r, carry):
            block(r, k, slot)
            return carry

        lax.fori_loop(low, high, one, 0)

    expand(0)
    row_copy(1, 0, 1).wait_recv()
    expand(1)
    blocks(0, 2, 0, 0)
    col_copy(1).wait_recv()
    prepare(1)
    blocks(0, 2, 1, 1)
    table_copy.wait()
    half = n_mem // 2 - 1

    def hand_on():
        col_copy(2).wait_recv()

        @pl.when(middle)
        def _():
            passed.start()

    def arrive(e, carry):
        if relay:
            @pl.when(e == min(2, half))
            def _():
                hand_on()

        r = 2 + 2 * (e % half) + e // half
        row_copy(r, 0, r).wait_recv()

        @pl.when(e < half)
        def _():
            row_copy(r + 1, r, 1).start()

        expand(r)

        def near(k, c2):
            block(r, k, k)
            return c2

        lax.fori_loop(0, 2, near, 0)
        return carry

    if half:
        lax.fori_loop(0, 2 * half, arrive, 0)
    elif relay:
        hand_on()
    finish(0, 0)
    finish(1, 1)

    def later(k, carry):
        if relay:
            @pl.when(k > 2)
            def _():
                col_copy(k).wait_recv()
        else:
            col_copy(k).wait_recv()
        prepare(k)
        blocks(0, n_mem, k, 0)
        finish(k, 0)
        return carry

    lax.fori_loop(2, n_grp, later, 0)

    for r in range(1, n_mem):
        row_copy(r, 0, r).wait_send()
    if relay:
        col_copy(1).wait_send()
        col_copy(2).wait_send()

        @pl.when(middle)
        def _():
            col_copy(3).wait_send()
            passed.wait_send()
    else:
        for k in range(1, n_grp):
            col_copy(k).wait_send()


def body(spectra, seg_mask, chan_pos):
    ch, segs, _, bins = spectra.shape
    n_grp, n_mem = lax.axis_size("grp"), lax.axis_size("mem")
    flat = spectra.reshape(-1, LANES)
    size = flat.shape[0] + META
    out = pl.pallas_call(
        functools.partial(kernel, n_grp, n_mem, ch, segs, bins, LAGS / (ch * n_grp * n_mem), math.sqrt(bins)),
        out_shape=jax.ShapeDtypeStruct((n_mem * ch, n_grp, ch, LAGS), jnp.bfloat16),
        in_specs=[
            pl.BlockSpec(memory_space=pltpu.VMEM),
            pl.BlockSpec(memory_space=pltpu.SMEM),
            pl.BlockSpec(memory_space=pltpu.SMEM),
            pl.BlockSpec(memory_space=pltpu.HBM),
        ],
        out_specs=pl.BlockSpec(memory_space=pltpu.VMEM),
        scratch_shapes=[
            pltpu.VMEM((n_mem, size, LANES), jnp.bfloat16),
            pltpu.VMEM((n_grp, size, LANES), jnp.bfloat16),
            pltpu.VMEM((n_grp, size, LANES), jnp.bfloat16),
            pltpu.VMEM((n_mem * ch * ch, LANES), jnp.float32),
            pltpu.VMEM((2 * n_mem * ch * ch * 2 * (bins // LANES), LANES), jnp.float32),
            pltpu.VMEM((2 * bins, LAGS), jnp.bfloat16),
            pltpu.SemaphoreType.DMA((n_mem,)),
            pltpu.SemaphoreType.DMA((n_mem,)),
            pltpu.SemaphoreType.DMA((n_grp,)),
            pltpu.SemaphoreType.DMA((n_grp,)),
            pltpu.SemaphoreType.DMA,
        ],
        compiler_params=pltpu.CompilerParams(
            collective_id=0, has_side_effects=True, vmem_limit_bytes=54528 * 1024),
    )(flat, seg_mask, chan_pos, jnp.asarray(make_table(bins, LAGS)))
    return out


def solution(mesh):
    in_specs = (P(("grp", "mem"), None, None, None), P(("grp", "mem"), None), P(("grp", "mem")))
    out_specs = P("grp", None, "mem", None)
    return jax.shard_map(body, mesh=mesh, in_specs=in_specs, out_specs=out_specs, check_vma=False)
```
